32 devices in a mesh: dp: 8 (over y, x, core), tensor: 4 (over z).
Axes of the slice: x: 2, y: 2, z: 4, core: 2. Of those that a mesh axis runs over, the one named last changes fastest.
Arguments:
- tokens: bfloat16 [4096, 768], P('dp'), may hold values from -6 to 6
- segment_ids: int32 [8, 512], P('dp'), may hold values from 0 to 1, never falling along the last dimension, each value on 1 to 320 neighbouring positions
- visible: int32 [8, 512], P('dp'), may hold values 0 or 1
- mask_index: int32 [8, 320], P('dp'), may hold values from 0 to 511, as said below
- targets: float32 [8, 320, 16], P('dp'), may hold values from -6 to 6
- noise: float32 [4, 8, 320, 16], P(None, 'dp'), may hold values from -6 to 6
- timesteps: int32 [4, 8, 320], P(None, 'dp'), may hold values from 1 to 998
- ln1_gain: float32 [768], replicated, may hold values from 0.5 to 1.5
- ln1_bias: float32 [768], replicated, may hold values from -3 to 3
- qkv_weight: bfloat16 [768, 3, 768], P(None, None, 'tensor'), may hold values from -0.21875 to 0.21875
- proj_weight: bfloat16 [768, 768], P('tensor'), may hold values from -1.75 to 1.75
- ln2_gain: float32 [768], replicated, may hold values from 0.5 to 1.5
- ln2_bias: float32 [768], replicated, may hold values from -3 to 3
- fc_in_weight: bfloat16 [768, 3072], P(None, 'tensor'), may hold values from -0.21875 to 0.21875
- fc_out_weight: bfloat16 [3072, 768], P('tensor'), may hold values from -0.109375 to 0.109375
- cond_weight: bfloat16 [768, 1024], replicated, may hold values from -0.21875 to 0.21875
- time_in_weight: bfloat16 [256, 1024], replicated, may hold values from -0.5 to 0.5
- time_out_weight: bfloat16 [1024, 1024], replicated, may hold values from -0.1875 to 0.1875
- input_weight: bfloat16 [16, 1024], P(None, 'tensor'), may hold values from -1.5 to 1.5
- ada_weight: bfloat16 [6, 1024, 3, 1024], P(None, None, None, 'tensor'), may hold values from -0.09375 to 0.09375
- block_in_weight: bfloat16 [6, 1024, 1024], P(None, None, 'tensor'), may hold values from -0.1875 to 0.1875
- block_out_weight: bfloat16 [6, 1024, 1024], P(None, 'tensor'), may hold values from -0.1875 to 0.1875
- final_ada_weight: bfloat16 [1024, 2, 1024], P(None, None, 'tensor'), may hold values from -0.09375 to 0.09375
- out_weight: bfloat16 [1024, 32], P('tensor'), may hold values from -0.1875 to 0.1875
Outputs:
- loss: float32 [], replicated
- hidden_out: bfloat16 [4096, 768], P('dp')
- input_grad: float32 [4096, 768], P('dp')
- ln1_gain_grad: float32 [768], replicated
- ln1_bias_grad: float32 [768], replicated
- qkv_grad: float32 [768, 3, 768], P('dp', None, 'tensor')
- proj_grad: float32 [768, 768], P('tensor', 'dp')
- ln2_gain_grad: float32 [768], replicated
- ln2_bias_grad: float32 [768], replicated
- fc_in_grad: float32 [768, 3072], P('dp', 'tensor')
- fc_out_grad: float32 [3072, 768], P('tensor', 'dp')
- cond_grad: float32 [768, 1024], P('dp')
- time_in_grad: float32 [256, 1024], P('dp')
- time_out_grad: float32 [1024, 1024], P('dp')
- input_weight_grad: float32 [16, 1024], P(None, 'tensor')
- ada_grad: float32 [6, 1024, 3, 1024], P(None, 'dp', None, 'tensor')
- block_in_grad: float32 [6, 1024, 1024], P(None, 'dp', 'tensor')
- block_out_grad: float32 [6, 1024, 1024], P(None, 'tensor', 'dp')
- final_ada_grad: float32 [1024, 2, 1024], P('dp', None, 'tensor')
- out_weight_grad: float32 [1024, 32], P('tensor')
The draws below stay inside these ranges and needn't reach their ends.
Inputs may be any that keep to these rules, and one draw needn't show every extreme that they name: `segment_ids`: within a row (one sequence) an image is a run of consecutive positions of at most 320 tokens, numbered in order. `mask_index`: each row holds 320 distinct positions of that sequence in increasing order.
All inputs are finite; a program needn't handle non-finite values. No bound on the sum of `visible` on one device may be relied on, other than what follows from the above.
Results may differ from the reference program's by a relative error of at most 0.02.
The reference program's roundings to bfloat16 on the way count: a program that leaves them out, or rounds other values in their place, can miss the bound.
Values may be sent and summed in bfloat16 or wider, within the bound.
A program may use at most 320 MiB of HBM per device.

```python
import math
import jax
import jax.numpy as jnp
import numpy as np
from jax import lax

D = 768
HEADS = 12
HEAD = 64
FF = 3072
HW = 1024
DEPTH = 6
TOKCH = 16
OUTCH = 32
FREQ = 256
COPIES = 4
STEPS = 1000
IMG = 320
TOK_DEV = 512
SEGS = 2
MASK_DEV = 320
SEQS = 8
TOKENS = 4096


def draw_mask_index(key, part):
    group_keys = jax.random.split(key, SEQS)

    def one_row(row_key):
        shuffled = jax.random.permutation(row_key, TOK_DEV)
        return jnp.sort(shuffled[:MASK_DEV])
    return jax.vmap(one_row)(group_keys).astype(jnp.int32)


def place_ends(result, own_key, low, largest):
    longest = result.shape.index(max(result.shape))
    spots = []
    for shift in (0, 1):
        where = [jax.random.randint(jax.random.fold_in(own_key, axis), (), 0, length) for axis, length in enumerate(result.shape)]
        where[longest] = (where[longest] + shift) % result.shape[longest]
        spots.append(tuple(where))
    return result.at[spots[0]].set(low).at[spots[1]].set(largest)


def levels(own_key, extent, cuts, low, largest):
    def one(dim, blocks):
        draws = jax.random.uniform(jax.random.fold_in(jax.random.fold_in(own_key, 6), dim), (blocks,), jnp.float32, low / len(cuts), largest / len(cuts))
        return jnp.repeat(jnp.exp(draws), extent[dim] // blocks).reshape((-1,) + (1,) * (len(extent) - dim - 1))

    factor_of = one(*cuts[0])
    for cut in cuts[1:]:
        factor_of = factor_of * one(*cut)
    return factor_of


def length_profile(count, total, bound, slope):
    loads = [(1 << 20) // math.isqrt(grade ** slope) + 1 for grade in range(2, count + 1)]
    surplus, given = total - bound - (count - 1), [1] * (count - 1)
    while surplus > 0:
        candidates = [i for i in range(count - 1) if given[i] < bound]
        mass, remaining = sum([loads[i] for i in candidates]), surplus
        for i in candidates:
            more = min(bound - given[i], max(1, remaining * loads[i] // mass), surplus)
            given[i] = given[i] + more
            surplus = surplus - more
    return np.array([bound] + given)


def ragged(key, number_of, total, bound, skew):
    if number_of == 2:
        one = jax.random.randint(key, (), max(1, total - bound), min(bound, total - 1) + 1)
        return jnp.stack([one, total - one])
    tallies = jnp.asarray(length_profile(number_of, total, bound, skew), jnp.int32)
    couples = (number_of - 1) // 2
    source_of, taker = tallies[1:1 + 2 * couples:2], tallies[2:2 + 2 * couples:2]
    room = jnp.minimum(source_of - 1, bound - taker)
    shifted = jax.random.randint(jax.random.fold_in(key, 1), (couples,), 0, 1 << 20) % (room + 1)
    tallies = tallies.at[1:1 + 2 * couples:2].set(source_of - shifted).at[2:2 + 2 * couples:2].set(taker + shifted)
    return tallies[jax.random.permutation(jax.random.fold_in(key, 2), number_of)]


def scatter_about(own_key, extent, deviation, limit, pieces=(), kind=jnp.bfloat16):
    level = levels(own_key, extent, pieces, -0.22, 0.18) if pieces else 1.0
    drawn = jax.random.normal(own_key, extent, jnp.float32) * deviation * level
    return jnp.minimum(jnp.maximum(drawn, -limit), limit).astype(kind)


def setup_inputs(seed: int = 0) -> dict:
    splits = jax.random.split(jax.random.key(seed), 25)
    return {
        "tokens": scatter_about(splits[0], (TOKENS, D), 1.0, 6.0, ((0, 8),)),
        "segment_ids": jax.vmap(lambda own: jnp.searchsorted(jnp.cumsum(ragged(own, SEGS, TOK_DEV, IMG, 2)), jnp.arange(TOK_DEV), side="right"))(jax.random.split(splits[1], SEQS)).reshape((SEQS, TOK_DEV)).astype(jnp.int32),
        "visible": place_ends((jax.random.randint(splits[2], (SEQS, TOK_DEV), 0, 4) < 3).astype(jnp.int32), jax.random.fold_in(splits[2], 1), 0, 1),
        "mask_index": draw_mask_index(jax.random.fold_in(splits[24], 71), 0),
        "targets": scatter_about(splits[4], (SEQS, MASK_DEV, TOKCH), 1.0, 6.0, ((0, 8),), jnp.float32),
        "noise": scatter_about(splits[5], (COPIES, SEQS, MASK_DEV, TOKCH), 1.0, 6.0, ((1, 8),), jnp.float32),
        "timesteps": place_ends(jax.random.randint(splits[6], (COPIES, SEQS, MASK_DEV), 1, STEPS - 1), jax.random.fold_in(splits[6], 1), 1, (STEPS - 1) - 1).astype(jnp.int32),
        "ln1_gain": jnp.clip(1.0 + 0.1 * jax.random.normal(splits[7], (D,), jnp.float32), 0.5, 1.5),
        "ln1_bias": scatter_about(splits[8], (D,), 0.3, 3.0, (), jnp.float32),
        "qkv_weight": scatter_about(splits[9], (D, 3, D), D ** -0.5, 0.21875, ((2, 4),)),
        "proj_weight": scatter_about(splits[10], (D, D), (max(1, D // 64)) ** -0.5, 1.75, ((0, 4),)),
        "ln2_gain": jnp.clip(1.0 + 0.1 * jax.random.normal(splits[11], (D,), jnp.float32), 0.5, 1.5),
        "ln2_bias": scatter_about(splits[12], (D,), 0.3, 3.0, (), jnp.float32),
        "fc_in_weight": scatter_about(splits[13], (D, FF), D ** -0.5, 0.21875, ((1, 4),)),
        "fc_out_weight": scatter_about(splits[14], (FF, D), FF ** -0.5, 0.109375, ((0, 4),)),
        "cond_weight": scatter_about(splits[15], (D, HW), D ** -0.5, 0.21875),
        "time_in_weight": scatter_about(splits[16], (FREQ, HW), (FREQ // 2) ** -0.5, 0.5),
        "time_out_weight": scatter_about(splits[17], (HW, HW), HW ** -0.5, 0.1875),
        "input_weight": scatter_about(splits[18], (TOKCH, HW), TOKCH ** -0.5, 1.5, ((1, 4),)),
        "ada_weight": scatter_about(splits[19], (DEPTH, HW, 3, HW), (4 * HW) ** -0.5, 0.09375, ((3, 4),)),
        "block_in_weight": scatter_about(splits[20], (DEPTH, HW, HW), HW ** -0.5, 0.1875, ((2, 4),)),
        "block_out_weight": scatter_about(splits[21], (DEPTH, HW, HW), HW ** -0.5, 0.1875, ((1, 4),)),
        "final_ada_weight": scatter_about(splits[22], (HW, 2, HW), (4 * HW) ** -0.5, 0.09375, ((2, 4),)),
        "out_weight": scatter_about(splits[23], (HW, OUTCH), HW ** -0.5, 0.1875, ((0, 4),)),
    }


@jax.custom_vjp
def low(v):
    return lax.optimization_barrier(v.astype(jnp.bfloat16)).astype(jnp.float32)

@jax.custom_vjp
def low_back(v):
    return v

def low_keep(v):
    return (low(v), None)

def low_pass(kept, grad):
    return (grad,)

def back_keep(v):
    return (v, None)

def back_low(kept, grad):
    return (low(grad),)
low.defvjp(low_keep, low_pass)
low_back.defvjp(back_keep, back_low)
norm_eps = 1e-06
highest = lax.Precision.HIGHEST

def matmul(left_op, right_op):
    return jnp.dot(left_op, right_op, precision=highest, preferred_element_type=jnp.float32)

def affine_norm(values, gain_vec, offset):
    centred = values - lax.optimization_barrier(jnp.mean(values, axis=-1, keepdims=True))
    spread = lax.optimization_barrier(jnp.mean(centred * centred, axis=-1, keepdims=True))
    return centred * lax.rsqrt(spread + norm_eps) * gain_vec + offset

def plain_norm(values):
    centred = values - lax.optimization_barrier(jnp.mean(values, axis=-1, keepdims=True))
    spread = lax.optimization_barrier(jnp.mean(centred * centred, axis=-1, keepdims=True))
    return centred * lax.rsqrt(spread + norm_eps)

def plan(time_rows):
    moment = time_rows.astype(jnp.float32)
    quarter = math.pi / 2.0
    angle_zero = 0.008 / 1.008 * quarter
    angle_now = ((moment + 1.0) / STEPS + 0.008) / 1.008 * quarter
    angle_prev = (moment / STEPS + 0.008) / 1.008 * quarter
    start_level = math.cos(angle_zero) ** 2
    abar_now = jnp.cos(angle_now) ** 2 / start_level
    abar_prev = jnp.cos(angle_prev) ** 2 / start_level
    one_minus_now = jnp.sin(angle_now - angle_zero) * jnp.sin(angle_now + angle_zero) / start_level
    one_minus_prev = jnp.sin(angle_prev - angle_zero) * jnp.sin(angle_prev + angle_zero) / start_level
    beta_step = jnp.sin(angle_now - angle_prev) * jnp.sin(angle_now + angle_prev) / jnp.cos(angle_prev) ** 2
    alpha_step = abar_now / abar_prev
    beta_tilde = beta_step * one_minus_prev / one_minus_now
    return (abar_now, alpha_step, beta_step, beta_tilde, one_minus_now)

def frequency(time_rows):
    half_width = FREQ // 2
    freq_rates = jnp.exp(-math.log(10000.0) * jnp.arange(half_width).astype(jnp.float32) / half_width)
    angles = time_rows.astype(jnp.float32)[:, None] * freq_rates[None, :]
    return jnp.concatenate([jnp.cos(angles), jnp.sin(angles)], axis=-1)

def loss_rows(predicted, eps_true, beta_step, beta_tilde, coef_diff):
    eps_pred = predicted[:, :TOKCH]
    var_raw = predicted[:, TOKCH:]
    squared = lax.optimization_barrier(jnp.mean((eps_true - eps_pred) ** 2, axis=-1))
    fraction = (var_raw + 1.0) / 2.0
    log_tilde = jnp.log(beta_tilde)
    log_model = fraction * jnp.log(beta_step) + (1.0 - fraction) * log_tilde
    mean_gap = coef_diff * (eps_pred - eps_true)
    diverge = 0.5 * (-1.0 + log_model - log_tilde + jnp.exp(log_tilde - log_model) + mean_gap * mean_gap * jnp.exp(-log_model))
    return squared + lax.optimization_barrier(jnp.mean(diverge, axis=-1)) / math.log(2.0)

def group_forward(token_rows, weights, segments, shown_keys, index_rows, start_in, noise_rows, time_rows):
    ln1_gain, ln1_bias, qkv_weight, proj_weight, ln2_gain, ln2_bias, fc_in_weight, fc_out_weight, cond_weight, time_in_weight, time_out_weight, input_weight, ada_weight, block_in_weight, block_out_weight, final_ada_weight, out_weight = weights
    token_count = token_rows.shape[0]
    attn_in = low(affine_norm(token_rows, ln1_gain, ln1_bias))
    projected = low(low_back(matmul(attn_in, qkv_weight.reshape(D, 3 * D)))).reshape(token_count, 3, HEADS, HEAD)
    queries = projected[:, 0]
    key_rows = projected[:, 1]
    value_rows = projected[:, 2]
    positions = jnp.arange(token_count)
    allowed = (segments[:, None] == segments[None, :]) & ((shown_keys[None, :] == 1) | (positions[:, None] == positions[None, :]))
    scores = jnp.einsum('qhd,khd->hqk', queries, key_rows, precision=highest) * (1.0 / math.sqrt(HEAD))
    scores = low_back(scores)
    scores = jnp.where(allowed[None], scores, -1e+30)
    probability = low(jax.nn.softmax(scores, axis=-1))
    attn_out = low(low_back(jnp.einsum('hqk,khd->qhd', probability, value_rows, precision=highest).reshape(token_count, D)))
    middle = token_rows + low_back(matmul(attn_out, proj_weight))
    mlp_in = low(affine_norm(middle, ln2_gain, ln2_bias))
    mlp_pre = low_back(matmul(mlp_in, fc_in_weight))
    activated = low(jax.nn.gelu(mlp_pre, approximate=False))
    hidden = middle + low_back(matmul(activated, fc_out_weight))
    cond_in = low(hidden)[index_rows]
    row_count = COPIES * MASK_DEV
    cond_pre = low_back(matmul(cond_in, cond_weight))
    time_flat = time_rows.reshape(row_count)
    embedded = low(frequency(time_flat))
    time_pre = low_back(matmul(embedded, time_in_weight))
    time_act = low(jax.nn.silu(time_pre))
    time_emb = low_back(matmul(time_act, time_out_weight))
    condition = (time_emb.reshape(COPIES, MASK_DEV, HW) + cond_pre[None]).reshape(row_count, HW)
    cond_act = low(jax.nn.silu(condition))
    abar_now, alpha_step, beta_step, beta_tilde, one_minus_now = plan(time_flat[:, None])
    start_rows = jnp.broadcast_to(start_in[None], (COPIES, MASK_DEV, TOKCH)).reshape(row_count, TOKCH)
    eps_true = noise_rows.reshape(row_count, TOKCH)
    noisy_rows = low(jnp.sqrt(abar_now) * start_rows + jnp.sqrt(one_minus_now) * eps_true)
    residual = low_back(matmul(noisy_rows, input_weight))
    for layer_index in range(DEPTH):
        modulation = low_back(matmul(cond_act, ada_weight[layer_index].reshape(HW, 3 * HW))).reshape(row_count, 3, HW)
        modulated = low(plain_norm(residual) * (1.0 + modulation[:, 1]) + modulation[:, 0])
        block_pre = low_back(matmul(modulated, block_in_weight[layer_index]))
        block_act = low(jax.nn.silu(block_pre))
        block_out = low_back(matmul(block_act, block_out_weight[layer_index]))
        residual = residual + modulation[:, 2] * block_out
    final_mod = low_back(matmul(cond_act, final_ada_weight.reshape(HW, 2 * HW))).reshape(row_count, 2, HW)
    final_in = low(plain_norm(residual) * (1.0 + final_mod[:, 1]) + final_mod[:, 0])
    predicted = low_back(matmul(final_in, out_weight))
    coef_diff = beta_step / jnp.sqrt(one_minus_now * alpha_step)
    row_loss = loss_rows(predicted, eps_true, beta_step, beta_tilde, coef_diff)
    return (jnp.sum(row_loss) / COPIES, (hidden, jnp.sum(row_loss)))

def reference(tokens, segment_ids, visible, mask_index, targets, noise, timesteps, ln1_gain, ln1_bias, qkv_weight, proj_weight, ln2_gain, ln2_bias, fc_in_weight, fc_out_weight, cond_weight, time_in_weight, time_out_weight, input_weight, ada_weight, block_in_weight, block_out_weight, final_ada_weight, out_weight):
    weights = tuple((weight.astype(jnp.float32) for weight in (ln1_gain, ln1_bias, qkv_weight, proj_weight, ln2_gain, ln2_bias, fc_in_weight, fc_out_weight, cond_weight, time_in_weight, time_out_weight, input_weight, ada_weight, block_in_weight, block_out_weight, final_ada_weight, out_weight)))
    token_groups = tokens.astype(jnp.float32).reshape(SEQS, TOK_DEV, D)
    noise_groups = jnp.transpose(noise, (1, 0, 2, 3))
    time_groups = jnp.transpose(timesteps, (1, 0, 2))

    def one_group(carry, group_data):
        token_rows, segments, shown_keys, index_rows, start_in, noise_rows, time_rows = group_data

        def objective(rows_in, weights_in):
            return group_forward(rows_in, weights_in, segments, shown_keys, index_rows, start_in, noise_rows, time_rows)
        total_value, back_fn, extras = jax.vjp(objective, token_rows, weights, has_aux=True)
        grad_rows, grad_weights = back_fn(jnp.ones_like(total_value))
        carry = jax.tree.map(lambda running, update: running + update, carry, grad_weights)
        return (carry, (extras[0], grad_rows, extras[1]))
    initial = jax.tree.map(jnp.zeros_like, weights)
    summed, (hidden, grads_in, losses) = lax.scan(one_group, initial, (token_groups, segment_ids, visible, mask_index, targets, noise_groups, time_groups))
    return (jnp.sum(losses) / (SEQS * COPIES * MASK_DEV), hidden.reshape(TOKENS, D).astype(jnp.bfloat16), grads_in.reshape(TOKENS, D), summed[0], summed[1], summed[2], summed[3], summed[4], summed[5], summed[6], summed[7], summed[8], summed[9], summed[10], summed[11], summed[12], summed[13], summed[14], summed[15], summed[16])
```

```python
from functools import partial
import math

import jax
import jax.numpy as jnp
from jax import lax
from jax.experimental import pallas as pl
from jax.experimental.pallas import tpu as pltpu
from jax.sharding import PartitionSpec as P

HEAD = 64
HW = 1024
DEPTH = 6
TOKCH = 16
FREQ = 256
COPIES = 4
STEPS = 1000

norm_eps = 1e-06
bf16 = jnp.bfloat16
f32 = jnp.float32


def product(left_op, right_op):
    return jnp.dot(left_op, right_op, preferred_element_type=f32)


def product_nt(left_op, right_op):
    return lax.dot_general(left_op, right_op, (((1,), (1,)), ((), ())), preferred_element_type=f32)


def product_tn(left_op, right_op):
    return lax.dot_general(left_op, right_op, (((0,), (0,)), ((), ())), preferred_element_type=f32)


def bit_list(size):
    bits = []
    while (1 << len(bits)) < size:
        bits.append(1 << len(bits))
    return bits


def flip(values, axis, mask):
    size = lax.axis_size(axis)
    return lax.ppermute(values, axis, [(i, i ^ mask) for i in range(size)])


def relabel(values, dim, count, own):
    step = values.shape[dim] // count
    return jnp.concatenate(
        [lax.dynamic_slice_in_dim(values, (own ^ r) * step, step, dim) for r in range(count)],
        axis=dim,
    )


def plain_norm(values):
    centred = values - jnp.mean(values, axis=-1, keepdims=True)
    inverse = lax.rsqrt(jnp.mean(centred * centred, axis=-1, keepdims=True) + norm_eps)
    return centred * inverse, inverse


def norm_back(grad_normal, normal, inverse):
    return inverse * (
        grad_normal
        - jnp.mean(grad_normal, axis=-1, keepdims=True)
        - normal * jnp.mean(grad_normal * normal, axis=-1, keepdims=True)
    )


def plan(time_rows):
    moment = time_rows.astype(f32)
    quarter = math.pi / 2.0
    angle_zero = 0.008 / 1.008 * quarter
    angle_now = ((moment + 1.0) / STEPS + 0.008) / 1.008 * quarter
    angle_prev = (moment / STEPS + 0.008) / 1.008 * quarter
    start_level = math.cos(angle_zero) ** 2
    abar_now = jnp.cos(angle_now) ** 2 / start_level
    abar_prev = jnp.cos(angle_prev) ** 2 / start_level
    one_minus_now = jnp.sin(angle_now - angle_zero) * jnp.sin(angle_now + angle_zero) / start_level
    one_minus_prev = (
        jnp.sin(angle_prev - angle_zero) * jnp.sin(angle_prev + angle_zero) / start_level
    )
    beta_step = (
        jnp.sin(angle_now - angle_prev) * jnp.sin(angle_now + angle_prev) / jnp.cos(angle_prev) ** 2
    )
    alpha_step = abar_now / abar_prev
    beta_tilde = beta_step * one_minus_prev / one_minus_now
    return (abar_now, alpha_step, beta_step, beta_tilde, one_minus_now)


def frequency(time_rows):
    half_width = FREQ // 2
    freq_rates = jnp.exp(-math.log(10000.0) * jnp.arange(half_width).astype(f32) / half_width)
    angles = time_rows.astype(f32)[:, None] * freq_rates[None, :]
    return jnp.concatenate([jnp.cos(angles), jnp.sin(angles)], axis=-1)


def loss_rows(predicted, eps_true, beta_step, beta_tilde, coef_diff):
    eps_pred = predicted[:, :TOKCH]
    var_raw = predicted[:, TOKCH:]
    squared = jnp.mean((eps_true - eps_pred) ** 2, axis=-1)
    fraction = (var_raw + 1.0) / 2.0
    log_tilde = jnp.log(beta_tilde)
    log_model = fraction * jnp.log(beta_step) + (1.0 - fraction) * log_tilde
    mean_gap = coef_diff * (eps_pred - eps_true)
    diverge = 0.5 * (
        -1.0
        + log_model
        - log_tilde
        + jnp.exp(log_tilde - log_model)
        + mean_gap * mean_gap * jnp.exp(-log_model)
    )
    return squared + jnp.mean(diverge, axis=-1) / math.log(2.0)


def gather_blocks(block):
    return [block] + [flip(block, "tensor", r) for r in range(1, lax.axis_size("tensor"))]


def scatter_sum(pieces):
    total = pieces[0].astype(f32)
    for r in range(1, len(pieces)):
        total = total + flip(pieces[r].astype(bf16), "tensor", r).astype(f32)
    return total


def gather_pack(chunk):
    full = lax.all_gather(chunk, ("dp", "tensor"), axis=0, tiled=False)
    return full.reshape((lax.axis_size("dp"), lax.axis_size("tensor")) + chunk.shape)


def reduce_pack(grads, z):
    part = lax.psum_scatter(grads, "dp", scatter_dimension=0, tiled=True)[0]
    return scatter_sum(
        [
            lax.dynamic_index_in_dim(part, z ^ r, axis=0, keepdims=False)
            for r in range(grads.shape[1])
        ]
    )


def reduce_outer(alive, order):
    for bit in order:
        going = sorted(k for k in alive if k & bit)
        sent = flip(jnp.stack([alive[k].astype(bf16) for k in going]), "dp", bit)
        alive = {
            k: alive[k] + sent[going.index(k | bit)].astype(f32) for k in alive if not k & bit
        }
    return alive[0]


def reduce_dp(keep, send):
    outer = bit_list(lax.axis_size("dp"))[1:]
    total = keep.astype(f32) + flip(send.astype(bf16), "dp", 1).astype(f32)
    return reduce_outer({2 * k: total[k] for k in range(total.shape[0])}, outer)


def reduce_halves(keep, send):
    outer = bit_list(lax.axis_size("dp"))[1:]
    total = keep.astype(f32) + flip(send, "dp", 1).astype(f32)
    half = keep.shape[1] // 2
    chunks = range(keep.shape[0])
    low = reduce_outer({2 * k: total[k, :half] for k in chunks}, outer)
    high = reduce_outer({2 * k: total[k, half:] for k in chunks}, outer[::-1])
    return scatter_sum([low[r] for r in range(half)] + [high[r] for r in range(half)])


VMEM_LIMIT = 60 * 1024 * 1024


def silu_pair(x):
    sig = 1.0 / (1.0 + jnp.exp(-x))
    return x * sig, sig * (1.0 + x * (1.0 - sig))


def weight(ref):
    n, _, _, c, w = ref.shape
    return ref[...].reshape(n * c, w)


def forward_kernel(
    resid_ref, cond_ref, a0_ref, a1_ref, a2_ref, in_ref, outw_ref,
    scale_ref, gate_ref, pre_ref, mod_ref, out_ref, next_ref, normal_s,
):
    s = pl.program_id(0)
    t = pl.num_programs(0) // 2
    hid = pre_ref.shape[1]

    @pl.when(s == 0)
    def _():
        normal_s[...] = plain_norm(resid_ref[...])[0]
        out_ref[...] = jnp.zeros_like(out_ref)

    @pl.when(s < t)
    def _():
        cond = cond_ref[...]
        cols = pl.ds(pl.multiple_of(s * hid, hid), hid)
        shift = product(cond, weight(a0_ref))
        scale = product(cond, weight(a1_ref))
        scale_ref[...] = scale
        gate_ref[:, cols] = product(cond, weight(a2_ref))
        mod_ref[:, cols] = (normal_s[:, cols] * (1.0 + scale) + shift).astype(bf16)

    @pl.when(s >= t)
    def _():
        pre = product(mod_ref[...], weight(in_ref))
        pre_ref[...] = pre
        out_ref[...] += product_nt(silu_pair(pre)[0].astype(bf16), weight(outw_ref))

    @pl.when(s == 2 * t - 1)
    def _():
        next_ref[...] = resid_ref[...] + gate_ref[...] * out_ref[...]


def whole(shape, dtype=None):
    return pl.BlockSpec(shape, lambda s: (0,) * len(shape), pipeline_mode=pl.Buffered(1))


def out_whole(shape):
    return pl.BlockSpec(shape, lambda s: (0,) * len(shape))


def params():
    return pltpu.CompilerParams(vmem_limit_bytes=VMEM_LIMIT)


def cost(flops, nbytes):
    return pl.CostEstimate(flops=int(flops), bytes_accessed=int(nbytes), transcendentals=0)


def pack_spec(pack, column, block):
    n, _, _, c, w = pack.shape
    return pl.BlockSpec((n, 1, 1, c, w), lambda s: (0, block(s), column, 0, 0))


def layer_forward(resid, cond, pack, first):
    rows = resid.shape[0]
    n, t, _, c, hid = pack.shape
    early = lambda s: jnp.minimum(s, t - 1)
    late = lambda s: jnp.maximum(s - t, 0)
    full = jax.ShapeDtypeStruct((rows, HW), f32)
    return pl.pallas_call(
        forward_kernel,
        grid=(2 * t,),
        in_specs=[whole((rows, HW)), whole((rows, HW))]
        + [pack_spec(pack, first + k, early) for k in range(3)]
        + [pack_spec(pack, first + k, late) for k in (3, 4)],
        out_specs=[
            pl.BlockSpec((rows, hid), lambda s: (0, early(s))),
            out_whole((rows, HW)),
            pl.BlockSpec((rows, hid), lambda s: (0, late(s))),
            out_whole((rows, HW)),
            out_whole((rows, HW)),
            out_whole((rows, HW)),
        ],
        out_shape=[full, full, full, jax.ShapeDtypeStruct((rows, HW), bf16), full, full],
        scratch_shapes=[pltpu.VMEM((rows, HW), f32)],
        compiler_params=params(),
        cost_estimate=cost(2 * rows * HW * 5 * HW, 10 * HW * HW + 30 * rows * HW),
    )(resid, cond, *[pack] * 5)


def backward_kernel(
    where_ref, gres_ref, resid_ref, scale_ref, gate_ref, out_ref, cond_ref, mod_ref, gc_ref, pre_ref,
    a0_ref, a1_ref, a2_ref, in_ref, outw_ref, *rest, split,
):
    if split:
        gnext_ref, gcn_ref, keep_ref, send_ref, normal_s, branch_s, gmi_s, dio_s = rest
        grad_ref = keep_ref
    else:
        gnext_ref, gcn_ref, grad_ref, normal_s, branch_s, gmi_s, dio_s = rest[-7:]
    s = pl.program_id(0)
    t = pl.num_programs(0) // 2
    hid = pre_ref.shape[1]
    d = where_ref[0]

    def put(k, value):
        c = grad_ref.shape[3]
        if not split:
            grad_ref[:, 0, k] = value.reshape(grad_ref.shape[0], c, hid)
            return
        value = value.reshape(2 * keep_ref.shape[0], c, hid)
        for parity in range(2):

            @pl.when((d & 1) == parity)
            def _():
                for chunk in range(value.shape[0]):
                    ref = keep_ref if (chunk & 1) == parity else send_ref
                    ref[(d ^ chunk) >> 1, 0, k] = value[chunk]

    @pl.when(s == 0)
    def _():
        branch_s[...] = (gate_ref[...] * gres_ref[...]).astype(bf16)
        gmi_s[...] = jnp.zeros_like(gmi_s)
        gcn_ref[...] = gc_ref[...]

    @pl.when(s < t)
    def _():
        grad_act = product(branch_s[...], weight(outw_ref))
        act, slope = silu_pair(pre_ref[...])
        grad_pre = (grad_act * slope).astype(bf16)
        gmi_s[...] += product_nt(grad_pre, weight(in_ref))
        dio_s[s, 0] = product_tn(mod_ref[...], grad_pre).astype(bf16)
        dio_s[s, 1] = product_tn(branch_s[...], act.astype(bf16)).astype(bf16)

    @pl.when(s == t - 1)
    def _():
        normal, inverse = plain_norm(resid_ref[...])
        normal_s[...] = normal
        gnext_ref[...] = gres_ref[...] + norm_back(
            gmi_s[...] * (1.0 + scale_ref[...]), normal, inverse
        )

    @pl.when(s >= t)
    def _():
        cols = pl.ds(pl.multiple_of((s - t) * hid, hid), hid)
        grad_mod_in = gmi_s[:, cols]
        grad_mods = (
            grad_mod_in.astype(bf16),
            (grad_mod_in * normal_s[:, cols]).astype(bf16),
            (gres_ref[:, cols] * out_ref[:, cols]).astype(bf16),
        )
        back = None
        for k, ref in enumerate((a0_ref, a1_ref, a2_ref)):
            put(k, product_tn(cond_ref[...], grad_mods[k]).astype(bf16))
            term = product_nt(grad_mods[k], weight(ref))
            back = term if back is None else back + term
        gcn_ref[...] += back
        for k in range(2):
            put(3 + k, dio_s[s - t, k])


def layer_backward(where, grad_resid, saved, cond, grad_cond, pack, first, grads, place, count):
    resid, scale, gate, pre, mod, out = saved
    rows = resid.shape[0]
    n, t, _, c, hid = pack.shape
    split = count == 0
    early = lambda s: jnp.minimum(s, t - 1)
    late = lambda s: jnp.maximum(s - t, 0)
    full = jax.ShapeDtypeStruct((rows, HW), f32)
    held = [] if grads is None else [grads]

    def resident(shape, **kw):
        return pl.BlockSpec(shape, lambda s, where: (0,) * len(shape), **kw)

    def weights(k, block):
        return pl.BlockSpec((n, 1, 1, c, hid), lambda s, where: (0, block(s), first + k, 0, 0))

    if split:
        pack_out = [
            pl.BlockSpec((n // 2, 1, 5, c, hid), lambda s, where: (0, late(s) ^ where[1], 0, 0, 0))
        ] * 2
        pack_shape = [jax.ShapeDtypeStruct((n // 2, t, 5, c, hid), bf16)] * 2
    else:
        pack_out = [
            pl.BlockSpec((n, 1, 5, c, hid), lambda s, where: (0, late(s), place, 0, 0))
        ]
        pack_shape = [jax.ShapeDtypeStruct((n, t, 5 * count, c, hid), bf16)]
    return pl.pallas_call(
        partial(backward_kernel, split=split),
        grid_spec=pltpu.PrefetchScalarGridSpec(
            num_scalar_prefetch=1,
            grid=(2 * t,),
            in_specs=[resident((rows, HW), pipeline_mode=pl.Buffered(1))] * 8
            + [pl.BlockSpec((rows, hid), lambda s, where: (0, early(s)))]
            + [weights(k, late) for k in range(3)]
            + [weights(k, early) for k in (3, 4)]
            + [pl.BlockSpec(memory_space=pl.ANY)] * len(held),
            out_specs=[resident((rows, HW)), resident((rows, HW))] + pack_out,
            scratch_shapes=[
                pltpu.VMEM((rows, HW), f32),
                pltpu.VMEM((rows, HW), bf16),
                pltpu.VMEM((rows, HW), f32),
                pltpu.VMEM((t, 2, HW, hid), bf16),
            ],
        ),
        out_shape=[full, full] + pack_shape,
        input_output_aliases={15: 2} if held else {},
        compiler_params=params(),
        cost_estimate=cost(4 * rows * HW * 5 * HW, 20 * HW * HW + 40 * rows * HW),
    )(where, grad_resid, resid, scale, gate, out, cond, mod, grad_cond, pre, *[pack] * 5, *held)


def final_kernel(
    resid_ref, cond_ref, eps_ref, coef_ref, wm_ref, wv_ref, f0_ref, f1_ref,
    gres_ref, gc_ref, grad_ref, loss_ref, dm_ref, dv_ref,
    scale_s, shift_s, normal_s, gfin_s,
):
    s = pl.program_id(0)
    t = pl.num_programs(0) // 2
    hid = f0_ref.shape[4]
    piece = (grad_ref.shape[0], grad_ref.shape[3], hid)

    @pl.when(s < t)
    def _():
        cols = pl.ds(pl.multiple_of(s * hid, hid), hid)
        shift_s[:, cols] = product(cond_ref[...], weight(f0_ref))
        scale_s[:, cols] = 1.0 + product(cond_ref[...], weight(f1_ref))

    @pl.when(s == t - 1)
    def _():
        normal, inverse = plain_norm(resid_ref[...])
        normal_s[...] = normal
        final_in = (normal * scale_s[...] + shift_s[...]).astype(bf16)
        eps_pred = product(final_in, wm_ref[...])
        var_raw = product(final_in, wv_ref[...])
        log_beta, log_tilde, coef = coef_ref[:, 0:1], coef_ref[:, 1:2], coef_ref[:, 2:3]
        miss = eps_pred - eps_ref[...]
        fraction = (var_raw + 1.0) / 2.0
        log_model = fraction * log_beta + (1.0 - fraction) * log_tilde
        mean_gap = coef * miss
        ratio = jnp.exp(log_tilde - log_model)
        precision = jnp.exp(-log_model)
        diverge = 0.5 * (
            -1.0 + log_model - log_tilde + ratio + mean_gap * mean_gap * precision
        )
        row_loss = jnp.mean(miss * miss, axis=-1, keepdims=True) + jnp.mean(
            diverge, axis=-1, keepdims=True
        ) / math.log(2.0)
        loss_ref[...] = jnp.broadcast_to(jnp.sum(row_loss, axis=0, keepdims=True), loss_ref.shape)
        share = 1.0 / (COPIES * TOKCH)
        grad_miss = (
            share * (2.0 * miss + mean_gap * precision * coef / math.log(2.0))
        ).astype(bf16)
        grad_var = (
            (share * 0.25 / math.log(2.0))
            * (1.0 - ratio - mean_gap * mean_gap * precision)
            * (log_beta - log_tilde)
        ).astype(bf16)
        dm_ref[...] = product_tn(final_in, grad_miss)
        dv_ref[...] = product_tn(final_in, grad_var)
        grad_fin = product_nt(grad_miss, wm_ref[...]) + product_nt(grad_var, wv_ref[...])
        gfin_s[...] = grad_fin
        gres_ref[...] = norm_back(grad_fin * scale_s[...], normal, inverse)
        gc_ref[...] = jnp.zeros_like(gc_ref)

    @pl.when(s >= t)
    def _():
        cols = pl.ds(pl.multiple_of((s - t) * hid, hid), hid)
        grad_fin = gfin_s[:, cols]
        grad_mods = (grad_fin.astype(bf16), (grad_fin * normal_s[:, cols]).astype(bf16))
        for k, ref in enumerate((f0_ref, f1_ref)):
            grad_ref[:, 0, k] = (
                product_tn(cond_ref[...], grad_mods[k]).astype(bf16).reshape(piece)
            )
            gc_ref[...] += product_nt(grad_mods[k], weight(ref))


def final_layer(resid, cond, eps_true, coefs, w_mean, w_var, pack, first):
    rows = resid.shape[0]
    n, t, _, c, hid = pack.shape
    full = jax.ShapeDtypeStruct((rows, HW), f32)
    thin = jax.ShapeDtypeStruct((HW, TOKCH), f32)
    both = lambda s: jnp.where(s < t, s, s - t)
    late = lambda s: jnp.maximum(s - t, 0)
    return pl.pallas_call(
        final_kernel,
        grid=(2 * t,),
        in_specs=[
            whole((rows, HW)),
            whole((rows, HW)),
            whole((rows, TOKCH)),
            whole((rows, 4)),
            whole((HW, TOKCH)),
            whole((HW, TOKCH)),
        ]
        + [pack_spec(pack, first + k, both) for k in range(2)],
        out_specs=[
            out_whole((rows, HW)),
            out_whole((rows, HW)),
            pl.BlockSpec((n, 1, 2, c, hid), lambda s: (0, late(s), 0, 0, 0)),
            out_whole((8, 128)),
            out_whole((HW, TOKCH)),
            out_whole((HW, TOKCH)),
        ],
        out_shape=[
            full,
            full,
            jax.ShapeDtypeStruct((n, t, 2, c, hid), bf16),
            jax.ShapeDtypeStruct((8, 128), f32),
            thin,
            thin,
        ],
        scratch_shapes=[pltpu.VMEM((rows, HW), f32)] * 4,
        compiler_params=params(),
        cost_estimate=cost(6 * rows * HW * 2 * HW, 8 * HW * HW + 20 * rows * HW),
    )(resid, cond, eps_true, coefs, w_mean, w_var, pack, pack)


def condition_kernel(
    emb_ref, in_ref, wti_ref, wto_ref, wc_ref, tpre_ref, tact_ref, condition_ref, cond_ref
):
    time_pre = product(emb_ref[...], wti_ref[...])
    tpre_ref[...] = time_pre
    time_act = silu_pair(time_pre)[0].astype(bf16)
    tact_ref[...] = time_act
    time_emb = product(time_act, wto_ref[...])
    cond_pre = product(in_ref[...], wc_ref[...])
    masked = in_ref.shape[0]
    for c in range(COPIES):
        rows = slice(c * masked, (c + 1) * masked)
        condition_ref[rows, :] = time_emb[rows] + cond_pre
    cond_ref[...] = silu_pair(condition_ref[...])[0].astype(bf16)


def vmem_spec():
    return pl.BlockSpec(memory_space=pltpu.VMEM)


def condition_forward(embedded, cond_in, time_in_weight, time_out_weight, cond_weight):
    rows = embedded.shape[0]
    full = jax.ShapeDtypeStruct((rows, HW), f32)
    low = jax.ShapeDtypeStruct((rows, HW), bf16)
    return pl.pallas_call(
        condition_kernel,
        in_specs=[vmem_spec()] * 5,
        out_specs=[vmem_spec()] * 4,
        out_shape=[full, low, full, low],
        compiler_params=params(),
        cost_estimate=cost(2 * rows * HW * 2 * HW, 4 * HW * HW + 10 * rows * HW),
    )(embedded, cond_in, time_in_weight, time_out_weight, cond_weight)


def condition_back_kernel(
    gc_ref, condition_ref, tpre_ref, tact_ref, emb_ref, in_ref, wto_ref, wc_ref,
    gin_ref, dto_ref, dti_ref, dc_ref, gcond_s,
):
    gcond_s[...] = gc_ref[...] * silu_pair(condition_ref[...])[1]
    grad_temb = gcond_s[...].astype(bf16)
    masked = in_ref.shape[0]
    total = gcond_s[0:masked, :]
    for c in range(1, COPIES):
        total = total + gcond_s[c * masked : (c + 1) * masked, :]
    grad_cpre = total.astype(bf16)
    gin_ref[...] = product_nt(grad_cpre, wc_ref[...]).astype(bf16)
    dc_ref[...] = product_tn(in_ref[...], grad_cpre).astype(bf16)
    grad_tact = product_nt(grad_temb, wto_ref[...])
    dto_ref[...] = product_tn(tact_ref[...], grad_temb).astype(bf16)
    grad_tpre = (grad_tact * silu_pair(tpre_ref[...])[1]).astype(bf16)
    dti_ref[...] = product_tn(emb_ref[...], grad_tpre).astype(bf16)


def condition_backward(
    grad_cond, condition, time_pre, time_act, embedded, cond_in, time_out_weight, cond_weight
):
    rows = embedded.shape[0]
    return pl.pallas_call(
        condition_back_kernel,
        in_specs=[vmem_spec()] * 8,
        out_specs=[vmem_spec()] * 4,
        out_shape=[
            jax.ShapeDtypeStruct(cond_in.shape, bf16),
            jax.ShapeDtypeStruct((HW, HW), bf16),
            jax.ShapeDtypeStruct((embedded.shape[1], HW), bf16),
            jax.ShapeDtypeStruct((cond_in.shape[1], HW), bf16),
        ],
        scratch_shapes=[pltpu.VMEM((rows, HW), f32)],
        compiler_params=params(),
        cost_estimate=cost(4 * rows * HW * 2 * HW, 10 * HW * HW + 20 * rows * HW),
    )(
        grad_cond, condition, time_pre, time_act, embedded, cond_in, time_out_weight,
        cond_weight,
    )


def butterfly(values, axis):
    for bit in bit_list(lax.axis_size(axis)):
        values = values + flip(values, axis, bit)
    return values


def shards(
    tokens,
    segment_ids,
    visible,
    mask_index,
    targets,
    noise,
    timesteps,
    ln1_gain,
    ln1_bias,
    qkv_weight,
    proj_weight,
    ln2_gain,
    ln2_bias,
    fc_in_weight,
    fc_out_weight,
    cond_weight,
    time_in_weight,
    time_out_weight,
    input_weight,
    ada_weight,
    block_in_weight,
    block_out_weight,
    final_ada_weight,
    out_weight,
):
    t, z = lax.axis_size("tensor"), lax.axis_index("tensor")
    n, d = lax.axis_size("dp"), lax.axis_index("dp")
    token_count, model_width = tokens.shape
    local_width = qkv_weight.shape[2]
    head_count = local_width // HEAD
    hid = input_weight.shape[1]
    chunk_rows = HW // n
    score_scale = 1.0 / math.sqrt(HEAD)
    own_rows = token_count // t

    ada_chunk = lax.dynamic_slice_in_dim(ada_weight, d * chunk_rows, chunk_rows, 1)
    in_chunk = lax.dynamic_slice_in_dim(block_in_weight, d * chunk_rows, chunk_rows, 1)
    out_chunk = lax.dynamic_slice_in_dim(block_out_weight, d * chunk_rows, chunk_rows, 2)
    def layer_chunk(l):
        return [
            jnp.moveaxis(ada_chunk[l], 1, 0),
            in_chunk[l][None],
            out_chunk[l].T[None],
        ]

    final_chunk = lax.dynamic_slice_in_dim(final_ada_weight, d * chunk_rows, chunk_rows, 0)
    half_depth = DEPTH // 2
    first_pack = gather_pack(
        jnp.concatenate(sum([layer_chunk(l) for l in range(half_depth)], []), axis=0)
    )
    second_pack = gather_pack(
        jnp.concatenate(
            sum([layer_chunk(l) for l in range(half_depth, DEPTH)], [])
            + [jnp.moveaxis(final_chunk, 1, 0)],
            axis=0,
        )
    )

    def pack_of(l):
        return (first_pack, 5 * l) if l < half_depth else (second_pack, 5 * (l - half_depth))

    input_full = relabel(jnp.concatenate(gather_blocks(input_weight), axis=1), 1, t, z)
    out_full = relabel(jnp.concatenate(gather_blocks(out_weight), axis=0), 0, t, z)

    inputs = relabel(tokens, 0, t, z).astype(f32)
    segments = relabel(segment_ids[0], 0, t, z)
    shown_keys = relabel(visible[0], 0, t, z)
    normal_one, inverse_one = plain_norm(inputs)
    attn_in = (normal_one * ln1_gain + ln1_bias).astype(bf16)
    qkv_flat = qkv_weight.reshape(model_width, 3 * local_width)
    projected = product(attn_in, qkv_flat).astype(bf16)
    queries = projected[:, :local_width].reshape(token_count, head_count, HEAD)
    key_rows = projected[:, local_width : 2 * local_width].reshape(token_count, head_count, HEAD)
    value_rows = projected[:, 2 * local_width :].reshape(token_count, head_count, HEAD)
    positions = jnp.arange(token_count)
    allowed = (segments[:, None] == segments[None, :]) & (
        (shown_keys[None, :] == 1) | (positions[:, None] == positions[None, :])
    )
    scores = (
        jnp.einsum("qhd,khd->hqk", queries, key_rows, preferred_element_type=f32) * score_scale
    )
    scores = jnp.where(allowed[None], scores, -1e30)
    row_top = jnp.max(scores, axis=-1, keepdims=True)
    weights_exp = jnp.exp(scores - row_top)
    row_total = jnp.sum(weights_exp, axis=-1, keepdims=True)
    probability = weights_exp / row_total
    prob_low = probability.astype(bf16)
    attn_out = (
        jnp.einsum("hqk,khd->qhd", prob_low, value_rows, preferred_element_type=f32)
        .reshape(token_count, local_width)
        .astype(bf16)
    )

    def row_blocks(values):
        return [values[r * own_rows : (r + 1) * own_rows] for r in range(t)]

    middle = inputs[:own_rows] + scatter_sum(row_blocks(product(attn_out, proj_weight)))
    normal_two, inverse_two = plain_norm(middle)
    mlp_in = jnp.concatenate(
        gather_blocks((normal_two * ln2_gain + ln2_bias).astype(bf16)), axis=0
    )
    mlp_pre = product(mlp_in, fc_in_weight)
    activated = jax.nn.gelu(mlp_pre, approximate=False).astype(bf16)
    hidden = middle + scatter_sum(row_blocks(product(activated, fc_out_weight)))
    hidden_rel = jnp.concatenate(gather_blocks(hidden.astype(bf16)), axis=0)
    hidden_out = relabel(hidden_rel, 0, t, z)

    masked_count = mask_index.shape[1]
    own_masked = masked_count // t
    row_count = COPIES * own_masked
    index_all = mask_index[0]
    index_all = ((index_all // own_rows) ^ z) * own_rows + index_all % own_rows
    index_all = relabel(index_all, 0, t, z)
    cond_in = hidden_rel[index_all[:own_masked]]
    time_own = lax.dynamic_slice_in_dim(timesteps[:, 0], z * own_masked, own_masked, 1)
    time_flat = time_own.reshape(row_count)
    embedded = frequency(time_flat).astype(bf16)
    time_pre, time_act, condition, cond_act = condition_forward(
        embedded, cond_in, time_in_weight, time_out_weight, cond_weight
    )
    abar_now, alpha_step, beta_step, beta_tilde, one_minus_now = plan(time_flat[:, None])
    start_own = lax.dynamic_slice_in_dim(targets[0], z * own_masked, own_masked, 0)
    start_rows = jnp.broadcast_to(start_own[None], (COPIES, own_masked, TOKCH)).reshape(
        row_count, TOKCH
    )
    eps_true = lax.dynamic_slice_in_dim(noise[:, 0], z * own_masked, own_masked, 1).reshape(
        row_count, TOKCH
    )
    noisy_rows = (jnp.sqrt(abar_now) * start_rows + jnp.sqrt(one_minus_now) * eps_true).astype(bf16)
    residual = product(noisy_rows, input_full)

    stored = []
    for l in range(DEPTH):
        scale, gate, pre, mod, block_out, following = layer_forward(
            residual, cond_act, *pack_of(l)
        )
        stored.append((residual, scale, gate, pre, mod, block_out))
        residual = following
    coef_diff = beta_step / jnp.sqrt(one_minus_now * alpha_step)
    coefs = jnp.concatenate(
        [jnp.log(beta_step), jnp.log(beta_tilde), coef_diff, jnp.zeros_like(coef_diff)], axis=1
    )

    grad_resid, grad_cact, final_grads, loss_tile, mean_part, var_part = final_layer(
        residual,
        cond_act,
        eps_true,
        coefs,
        out_full[:, :TOKCH],
        out_full[:, TOKCH:],
        second_pack,
        5 * (DEPTH - half_depth),
    )
    loss_total = loss_tile[0, 0]
    out_weight_part = jnp.concatenate([mean_part, var_part], axis=1)

    final_grad = jnp.moveaxis(reduce_pack(final_grads, z), 0, 1)
    where = jnp.stack([d, z]).astype(jnp.int32)
    reds = [None] * DEPTH
    grads = None
    for l in reversed(range(half_depth, DEPTH)):
        grad_resid, grad_cact, grads = layer_backward(
            where, grad_resid, stored[l], cond_act, grad_cact, *pack_of(l),
            grads, l - half_depth, DEPTH - half_depth,
        )
    summed = reduce_pack(grads, z)
    for l in range(half_depth, DEPTH):
        reds[l] = summed[5 * (l - half_depth) : 5 * (l - half_depth) + 5]
    for l in reversed(range(half_depth)):
        grad_resid, grad_cact, keep, send = layer_backward(
            where, grad_resid, stored[l], cond_act, grad_cact, *pack_of(l), None, 0, 0
        )
        reds[l] = reduce_halves(keep, send)
    ada_grad = jnp.stack([jnp.moveaxis(red[:3], 0, 1) for red in reds])
    in_grad = jnp.stack([red[3] for red in reds])
    out_grad = jnp.stack([red[4].T for red in reds])
    input_weight_part = product_tn(noisy_rows, grad_resid.astype(bf16))

    grad_cond_in, *thin = condition_backward(
        grad_cact, condition, time_pre, time_act, embedded, cond_in, time_out_weight, cond_weight
    )
    thin = jnp.concatenate([part.reshape(n, part.shape[0] // n, HW) for part in thin], axis=1)
    thin = relabel(thin, 0, n, d)
    thin_red = reduce_dp(thin[::2], thin[1::2])
    for bit in bit_list(t):
        thin_low = thin_red.astype(bf16)
        thin_red = thin_low.astype(f32) + flip(thin_low, "tensor", bit).astype(f32)
    marks = [HW // n, HW // n + FREQ // n]
    time_out_grad, time_in_grad, cond_grad = jnp.split(thin_red, marks, axis=0)

    grad_in_all = jnp.concatenate(gather_blocks(grad_cond_in), axis=0)
    grad_mlp = jnp.zeros((token_count, model_width), bf16).at[index_all].add(grad_in_all)
    grad_act_mlp = product_nt(grad_mlp, fc_out_weight)
    grad_mlp_pre = jax.vjp(partial(jax.nn.gelu, approximate=False), mlp_pre)[1](grad_act_mlp)[
        0
    ].astype(bf16)
    grad_normed_two = scatter_sum(row_blocks(product_nt(grad_mlp_pre, fc_in_weight)))
    ln2_gain_part = jnp.sum(grad_normed_two * normal_two, axis=0)
    ln2_bias_part = jnp.sum(grad_normed_two, axis=0)
    grad_middle = grad_mlp[:own_rows].astype(f32) + norm_back(
        grad_normed_two * ln2_gain, normal_two, inverse_two
    )
    grad_attn = jnp.concatenate(gather_blocks(grad_middle.astype(bf16)), axis=0)
    grad_attn_out = (
        product_nt(grad_attn, proj_weight).astype(bf16).reshape(token_count, head_count, HEAD)
    )
    value_grad = jnp.einsum("hqk,qhd->khd", prob_low, grad_attn_out, preferred_element_type=f32)
    grad_prob = jnp.einsum("qhd,khd->hqk", grad_attn_out, value_rows, preferred_element_type=f32)
    row_delta = jnp.sum(probability * grad_prob, axis=-1, keepdims=True)
    grad_scores = (probability * (grad_prob - row_delta)).astype(bf16)
    query_grad = (
        jnp.einsum("hqk,khd->qhd", grad_scores, key_rows, preferred_element_type=f32) * score_scale
    )
    key_grad = (
        jnp.einsum("hqk,qhd->khd", grad_scores, queries, preferred_element_type=f32) * score_scale
    )
    grad_qkv = jnp.concatenate(
        [
            query_grad.reshape(token_count, local_width),
            key_grad.reshape(token_count, local_width),
            value_grad.reshape(token_count, local_width),
        ],
        axis=1,
    ).astype(bf16)
    grad_normed_one = scatter_sum(row_blocks(product_nt(grad_qkv, qkv_flat)))
    own_normal = normal_one[:own_rows]
    ln1_gain_part = jnp.sum(grad_normed_one * own_normal, axis=0)
    ln1_bias_part = jnp.sum(grad_normed_one, axis=0)
    input_own = grad_middle + norm_back(
        grad_normed_one * ln1_gain, own_normal, inverse_one[:own_rows]
    )
    input_grad = relabel(
        jnp.concatenate(gather_blocks(input_own.astype(bf16)), axis=0), 0, t, z
    ).astype(f32)

    whole_grads = jnp.concatenate(
        [
            product_tn(attn_in, grad_qkv),
            product_tn(grad_attn, attn_out),
            product_tn(mlp_in, grad_mlp_pre),
            product_tn(grad_mlp, activated),
        ],
        axis=1,
    )
    whole_grads = relabel(
        whole_grads.astype(bf16).reshape(n, model_width // n, whole_grads.shape[1]), 0, n, d
    )
    block_red = reduce_dp(whole_grads[::2], whole_grads[1::2])
    marks = [3 * local_width, 4 * local_width, 4 * local_width + fc_in_weight.shape[1]]
    qkv_red, proj_red, fc_in_red, fc_out_red = jnp.split(block_red, marks, axis=1)

    lane_parts = jnp.concatenate(
        [
            ln1_gain_part,
            ln1_bias_part,
            ln2_gain_part,
            ln2_bias_part,
            jnp.full((128,), loss_total, f32),
        ]
    )
    input_weight_part = relabel(input_weight_part, 1, t, z)
    out_weight_part = relabel(out_weight_part, 0, t, z)
    shard_parts = [
        jnp.concatenate(
            [
                input_weight_part[:, r * hid : (r + 1) * hid].reshape(-1),
                out_weight_part[r * hid : (r + 1) * hid].reshape(-1),
            ]
        )
        for r in range(t)
    ]
    shard_own = shard_parts[0]
    for r in range(1, t):
        shard_own = shard_own + flip(shard_parts[r], "tensor", r)
    small = butterfly(jnp.concatenate([butterfly(lane_parts, "tensor"), shard_own]), "dp")
    lanes = 4 * model_width + 128
    edge = lanes + TOKCH * hid
    loss_mean = small[4 * model_width] / (n * t * row_count)
    return (
        loss_mean,
        hidden_out,
        input_grad,
        small[:model_width],
        small[model_width : 2 * model_width],
        qkv_red.reshape(model_width // n, 3, local_width),
        proj_red.T,
        small[2 * model_width : 3 * model_width],
        small[3 * model_width : 4 * model_width],
        fc_in_red,
        fc_out_red.T,
        cond_grad,
        time_in_grad,
        time_out_grad,
        small[lanes:edge].reshape(TOKCH, hid),
        ada_grad,
        in_grad,
        out_grad,
        final_grad,
        small[edge:].reshape(out_weight.shape),
    )


def solution(mesh):
    placed = (
        P("dp", None),
        P("dp", None),
        P("dp", None),
        P("dp", None),
        P("dp", None, None),
        P(None, "dp", None, None),
        P(None, "dp", None),
        P(),
        P(),
        P(None, None, "tensor"),
        P("tensor", None),
        P(),
        P(),
        P(None, "tensor"),
        P("tensor", None),
        P(),
        P(),
        P(),
        P(None, "tensor"),
        P(None, None, None, "tensor"),
        P(None, None, "tensor"),
        P(None, "tensor", None),
        P(None, None, "tensor"),
        P("tensor", None),
    )
    return jax.shard_map(
        shards,
        mesh=mesh,
        in_specs=placed,
        out_specs=(
            P(),
            P("dp", None),
            P("dp", None),
            P(),
            P(),
            P("dp", None, "tensor"),
            P("tensor", "dp"),
            P(),
            P(),
            P("dp", "tensor"),
            P("tensor", "dp"),
            P("dp", None),
            P("dp", None),
            P("dp", None),
            P(None, "tensor"),
            P(None, "dp", None, "tensor"),
            P(None, "dp", "tensor"),
            P(None, "tensor", "dp"),
            P("dp", None, "tensor"),
            P("tensor", None),
        ),
        check_vma=False,
    )
```

```python
from functools import partial
import math

import jax
import jax.numpy as jnp
from jax import lax
from jax.experimental import pallas as pl
from jax.experimental.pallas import tpu as pltpu
from jax.sharding import PartitionSpec as P

HEAD = 64
HW = 1024
DEPTH = 6
TOKCH = 16
FREQ = 256
COPIES = 4
STEPS = 1000
GROUPS = ((5, 4, 3), (2, 1, 0))

norm_eps = 1e-06
bf16 = jnp.bfloat16
f32 = jnp.float32


def product(left_op, right_op):
    return jnp.dot(left_op, right_op, preferred_element_type=f32)


def product_nt(left_op, right_op):
    return lax.dot_general(left_op, right_op, (((1,), (1,)), ((), ())), preferred_element_type=f32)


def product_tn(left_op, right_op):
    return lax.dot_general(left_op, right_op, (((0,), (0,)), ((), ())), preferred_element_type=f32)


def bit_list(size):
    bits = []
    while (1 << len(bits)) < size:
        bits.append(1 << len(bits))
    return bits


def flip(values, axis, mask):
    size = lax.axis_size(axis)
    return lax.ppermute(values, axis, [(i, i ^ mask) for i in range(size)])


def relabel(values, dim, count, own):
    step = values.shape[dim] // count
    return jnp.concatenate(
        [lax.dynamic_slice_in_dim(values, (own ^ r) * step, step, dim) for r in range(count)],
        axis=dim,
    )


def plain_norm(values):
    centred = values - jnp.mean(values, axis=-1, keepdims=True)
    inverse = lax.rsqrt(jnp.mean(centred * centred, axis=-1, keepdims=True) + norm_eps)
    return centred * inverse, inverse


def norm_back(grad_normal, normal, inverse):
    return inverse * (
        grad_normal
        - jnp.mean(grad_normal, axis=-1, keepdims=True)
        - normal * jnp.mean(grad_normal * normal, axis=-1, keepdims=True)
    )


def plan(time_rows):
    moment = time_rows.astype(f32)
    quarter = math.pi / 2.0
    angle_zero = 0.008 / 1.008 * quarter
    angle_now = ((moment + 1.0) / STEPS + 0.008) / 1.008 * quarter
    angle_prev = (moment / STEPS + 0.008) / 1.008 * quarter
    start_level = math.cos(angle_zero) ** 2
    abar_now = jnp.cos(angle_now) ** 2 / start_level
    abar_prev = jnp.cos(angle_prev) ** 2 / start_level
    one_minus_now = jnp.sin(angle_now - angle_zero) * jnp.sin(angle_now + angle_zero) / start_level
    one_minus_prev = (
        jnp.sin(angle_prev - angle_zero) * jnp.sin(angle_prev + angle_zero) / start_level
    )
    beta_step = (
        jnp.sin(angle_now - angle_prev) * jnp.sin(angle_now + angle_prev) / jnp.cos(angle_prev) ** 2
    )
    alpha_step = abar_now / abar_prev
    beta_tilde = beta_step * one_minus_prev / one_minus_now
    return (abar_now, alpha_step, beta_step, beta_tilde, one_minus_now)


def frequency(time_rows):
    half_width = FREQ // 2
    freq_rates = jnp.exp(-math.log(10000.0) * jnp.arange(half_width).astype(f32) / half_width)
    angles = time_rows.astype(f32)[:, None] * freq_rates[None, :]
    return jnp.concatenate([jnp.cos(angles), jnp.sin(angles)], axis=-1)


def loss_rows(predicted, eps_true, beta_step, beta_tilde, coef_diff):
    eps_pred = predicted[:, :TOKCH]
    var_raw = predicted[:, TOKCH:]
    squared = jnp.mean((eps_true - eps_pred) ** 2, axis=-1)
    fraction = (var_raw + 1.0) / 2.0
    log_tilde = jnp.log(beta_tilde)
    log_model = fraction * jnp.log(beta_step) + (1.0 - fraction) * log_tilde
    mean_gap = coef_diff * (eps_pred - eps_true)
    diverge = 0.5 * (
        -1.0
        + log_model
        - log_tilde
        + jnp.exp(log_tilde - log_model)
        + mean_gap * mean_gap * jnp.exp(-log_model)
    )
    return squared + jnp.mean(diverge, axis=-1) / math.log(2.0)


def gather_blocks(block):
    return [block] + [flip(block, "tensor", r) for r in range(1, lax.axis_size("tensor"))]


def scatter_sum(pieces):
    total = pieces[0].astype(f32)
    for r in range(1, len(pieces)):
        total = total + flip(pieces[r].astype(bf16), "tensor", r).astype(f32)
    return total


def gather_pack(chunk):
    full = lax.all_gather(chunk, ("dp", "tensor"), axis=0, tiled=False)
    return full.reshape((lax.axis_size("dp"), lax.axis_size("tensor")) + chunk.shape)


def reduce_over_dp(grads):
    return lax.psum_scatter(grads, "dp", scatter_dimension=0, tiled=True)[0]


def reduce_tensor(part, z):
    return scatter_sum(
        [
            lax.dynamic_index_in_dim(part, z ^ r, axis=0, keepdims=False)
            for r in range(part.shape[0])
        ]
    )


def after(value, *arrived):
    return lax.optimization_barrier((value,) + arrived)[0]


def reduce_outer(alive, order):
    for bit in order:
        going = sorted(k for k in alive if k & bit)
        sent = flip(jnp.stack([alive[k].astype(bf16) for k in going]), "dp", bit)
        alive = {
            k: alive[k] + sent[going.index(k | bit)].astype(f32) for k in alive if not k & bit
        }
    return alive[0]


def reduce_dp(keep, send):
    outer = bit_list(lax.axis_size("dp"))[1:]
    total = keep.astype(f32) + flip(send.astype(bf16), "dp", 1).astype(f32)
    return reduce_outer({2 * k: total[k] for k in range(total.shape[0])}, outer)


VMEM_LIMIT = 60 * 1024 * 1024


def silu_pair(x):
    sig = 1.0 / (1.0 + jnp.exp(-x))
    return x * sig, sig * (1.0 + x * (1.0 - sig))


def weight(ref):
    n, _, _, c, w = ref.shape
    return ref[...].reshape(n * c, w)


def forward_kernel(
    resid_ref, cond_ref, a0_ref, a1_ref, a2_ref, in_ref, outw_ref,
    scale_ref, gate_ref, pre_ref, mod_ref, out_ref, next_ref, normal_s,
):
    s = pl.program_id(0)
    t = pl.num_programs(0) // 2
    hid = pre_ref.shape[1]

    @pl.when(s == 0)
    def _():
        normal_s[...] = plain_norm(resid_ref[...])[0]
        out_ref[...] = jnp.zeros_like(out_ref)

    @pl.when(s < t)
    def _():
        cond = cond_ref[...]
        cols = pl.ds(pl.multiple_of(s * hid, hid), hid)
        shift = product(cond, weight(a0_ref))
        scale = product(cond, weight(a1_ref))
        scale_ref[...] = scale
        gate_ref[:, cols] = product(cond, weight(a2_ref))
        mod_ref[:, cols] = (normal_s[:, cols] * (1.0 + scale) + shift).astype(bf16)

    @pl.when(s >= t)
    def _():
        pre = product(mod_ref[...], weight(in_ref))
        pre_ref[...] = pre
        out_ref[...] += product_nt(silu_pair(pre)[0].astype(bf16), weight(outw_ref))

    @pl.when(s == 2 * t - 1)
    def _():
        next_ref[...] = resid_ref[...] + gate_ref[...] * out_ref[...]


def whole(shape, dtype=None):
    return pl.BlockSpec(shape, lambda s: (0,) * len(shape), pipeline_mode=pl.Buffered(1))


def out_whole(shape):
    return pl.BlockSpec(shape, lambda s: (0,) * len(shape))


def params():
    return pltpu.CompilerParams(vmem_limit_bytes=VMEM_LIMIT)


def cost(flops, nbytes):
    return pl.CostEstimate(flops=int(flops), bytes_accessed=int(nbytes), transcendentals=0)


def pack_spec(pack, column, block):
    n, _, _, c, w = pack.shape
    return pl.BlockSpec((n, 1, 1, c, w), lambda s: (0, block(s), column, 0, 0))


def layer_forward(resid, cond, pack, first):
    rows = resid.shape[0]
    n, t, _, c, hid = pack.shape
    early = lambda s: jnp.minimum(s, t - 1)
    late = lambda s: jnp.maximum(s - t, 0)
    full = jax.ShapeDtypeStruct((rows, HW), f32)
    return pl.pallas_call(
        forward_kernel,
        grid=(2 * t,),
        in_specs=[whole((rows, HW)), whole((rows, HW))]
        + [pack_spec(pack, first + k, early) for k in range(3)]
        + [pack_spec(pack, first + k, late) for k in (3, 4)],
        out_specs=[
            pl.BlockSpec((rows, hid), lambda s: (0, early(s))),
            out_whole((rows, HW)),
            pl.BlockSpec((rows, hid), lambda s: (0, late(s))),
            out_whole((rows, HW)),
            out_whole((rows, HW)),
            out_whole((rows, HW)),
        ],
        out_shape=[full, full, full, jax.ShapeDtypeStruct((rows, HW), bf16), full, full],
        scratch_shapes=[pltpu.VMEM((rows, HW), f32)],
        compiler_params=params(),
        cost_estimate=cost(2 * rows * HW * 5 * HW, 10 * HW * HW + 30 * rows * HW),
    )(resid, cond, *[pack] * 5)


def backward_kernel(
    gres_ref, resid_ref, scale_ref, gate_ref, out_ref, turned_ref, mod_ref, gc_ref, pre_ref,
    a0_ref, a1_ref, a2_ref, in_ref, outw_ref, *rest,
):
    gnext_ref, gcn_ref, grad_ref, normal_s, branch_s, gmi_s, dio_s, modt_s, brancht_s = rest[-9:]
    s = pl.program_id(0)
    t = pl.num_programs(0) // 2
    hid = pre_ref.shape[1]
    piece = (grad_ref.shape[0], grad_ref.shape[3], hid)

    @pl.when(s == 0)
    def _():
        branch = gate_ref[...] * gres_ref[...]
        branch_s[...] = branch.astype(bf16)
        brancht_s[...] = branch.astype(bf16).T
        modt_s[...] = mod_ref[...].T
        gmi_s[...] = jnp.zeros_like(gmi_s)
        gcn_ref[...] = gc_ref[...]

    @pl.when(s < t)
    def _():
        grad_act = product(branch_s[...], weight(outw_ref))
        act, slope = silu_pair(pre_ref[...])
        grad_pre = (grad_act * slope).astype(bf16)
        gmi_s[...] += product_nt(grad_pre, weight(in_ref))
        dio_s[s, 0] = product(modt_s[...], grad_pre).astype(bf16)
        dio_s[s, 1] = product(brancht_s[...], act.astype(bf16)).astype(bf16)

    @pl.when(s == t - 1)
    def _():
        normal, inverse = plain_norm(resid_ref[...])
        normal_s[...] = normal
        gnext_ref[...] = gres_ref[...] + norm_back(
            gmi_s[...] * (1.0 + scale_ref[...]), normal, inverse
        )

    @pl.when(s >= t)
    def _():
        cols = pl.ds(pl.multiple_of((s - t) * hid, hid), hid)
        grad_mod_in = gmi_s[:, cols]
        grad_mods = (
            grad_mod_in.astype(bf16),
            (grad_mod_in * normal_s[:, cols]).astype(bf16),
            (gres_ref[:, cols] * out_ref[:, cols]).astype(bf16),
        )
        back = None
        for k, ref in enumerate((a0_ref, a1_ref, a2_ref)):
            grad_ref[:, 0, k] = product(turned_ref[...], grad_mods[k]).astype(bf16).reshape(piece)
            term = product_nt(grad_mods[k], weight(ref))
            back = term if back is None else back + term
        gcn_ref[...] += back
        for k in range(2):
            grad_ref[:, 0, 3 + k] = dio_s[s - t, k].reshape(piece)


def layer_backward(grad_resid, saved, turned, grad_cond, pack, first, grads, place, count):
    resid, scale, gate, pre, mod, out = saved
    rows = resid.shape[0]
    n, t, _, c, hid = pack.shape
    early = lambda s: jnp.minimum(s, t - 1)
    late = lambda s: jnp.maximum(s - t, 0)
    full = jax.ShapeDtypeStruct((rows, HW), f32)
    held = [] if grads is None else [grads]
    blocks = 5 * count if grads is None else grads.shape[2]
    return pl.pallas_call(
        backward_kernel,
        grid=(2 * t,),
        in_specs=[whole((rows, HW))] * 5
        + [whole((HW, rows))]
        + [whole((rows, HW))] * 2
        + [pl.BlockSpec((rows, hid), lambda s: (0, early(s)))]
        + [pack_spec(pack, first + k, late) for k in range(3)]
        + [pack_spec(pack, first + k, early) for k in (3, 4)]
        + [pl.BlockSpec(memory_space=pl.ANY)] * len(held),
        out_specs=[
            out_whole((rows, HW)),
            out_whole((rows, HW)),
            pl.BlockSpec((n, 1, 5, c, hid), lambda s: (0, late(s), place, 0, 0)),
        ],
        out_shape=[full, full, jax.ShapeDtypeStruct((n, t, blocks, c, hid), bf16)],
        input_output_aliases={14: 2} if held else {},
        scratch_shapes=[
            pltpu.VMEM((rows, HW), f32),
            pltpu.VMEM((rows, HW), bf16),
            pltpu.VMEM((rows, HW), f32),
            pltpu.VMEM((t, 2, HW, hid), bf16),
            pltpu.VMEM((HW, rows), bf16),
            pltpu.VMEM((HW, rows), bf16),
        ],
        compiler_params=params(),
        cost_estimate=cost(rows, rows),
    )(grad_resid, resid, scale, gate, out, turned, mod, grad_cond, pre, *[pack] * 5, *held)


def final_kernel(
    resid_ref, cond_ref, eps_ref, coef_ref, wm_ref, wv_ref, f0_ref, f1_ref, fb_ref,
    gres_ref, gc_ref, grad_ref, loss_ref, dm_ref, dv_ref,
    scale_s, shift_s, normal_s, gfin_s,
):
    s = pl.program_id(0)
    t = pl.num_programs(0) // 3
    hid = f0_ref.shape[4]
    piece = (grad_ref.shape[0], grad_ref.shape[3], hid)

    @pl.when(s < t)
    def _():
        cols = pl.ds(pl.multiple_of(s * hid, hid), hid)
        shift_s[:, cols] = product(cond_ref[...], weight(f0_ref))
        scale_s[:, cols] = 1.0 + product(cond_ref[...], weight(f1_ref))

    @pl.when(s == t - 1)
    def _():
        normal, inverse = plain_norm(resid_ref[...])
        normal_s[...] = normal
        final_in = (normal * scale_s[...] + shift_s[...]).astype(bf16)
        eps_pred = product(final_in, wm_ref[...])
        var_raw = product(final_in, wv_ref[...])
        log_beta, log_tilde, coef = coef_ref[:, 0:1], coef_ref[:, 1:2], coef_ref[:, 2:3]
        miss = eps_pred - eps_ref[...]
        fraction = (var_raw + 1.0) / 2.0
        log_model = fraction * log_beta + (1.0 - fraction) * log_tilde
        mean_gap = coef * miss
        ratio = jnp.exp(log_tilde - log_model)
        precision = jnp.exp(-log_model)
        diverge = 0.5 * (
            -1.0 + log_model - log_tilde + ratio + mean_gap * mean_gap * precision
        )
        row_loss = jnp.mean(miss * miss, axis=-1, keepdims=True) + jnp.mean(
            diverge, axis=-1, keepdims=True
        ) / math.log(2.0)
        loss_ref[...] = jnp.broadcast_to(jnp.sum(row_loss, axis=0, keepdims=True), loss_ref.shape)
        share = 1.0 / (COPIES * TOKCH)
        grad_miss = (
            share * (2.0 * miss + mean_gap * precision * coef / math.log(2.0))
        ).astype(bf16)
        grad_var = (
            (share * 0.25 / math.log(2.0))
            * (1.0 - ratio - mean_gap * mean_gap * precision)
            * (log_beta - log_tilde)
        ).astype(bf16)
        dm_ref[...] = product_tn(final_in, grad_miss)
        dv_ref[...] = product_tn(final_in, grad_var)
        grad_fin = product_nt(grad_miss, wm_ref[...]) + product_nt(grad_var, wv_ref[...])
        gfin_s[...] = grad_fin
        gres_ref[...] = norm_back(grad_fin * scale_s[...], normal, inverse)
        gc_ref[...] = jnp.zeros_like(gc_ref)

    @pl.when(s >= t)
    def _():
        cols = pl.ds(pl.multiple_of(((s - t) >> 1) * hid, hid), hid)
        factor = jnp.where(((s - t) & 1) == 0, 1.0, normal_s[:, cols])
        grad_mod = (gfin_s[:, cols] * factor).astype(bf16)
        grad_ref[:, 0, 0] = product_tn(cond_ref[...], grad_mod).astype(bf16).reshape(piece)
        gc_ref[...] += product_nt(grad_mod, weight(fb_ref))


def final_layer(resid, cond, eps_true, coefs, w_mean, w_var, pack, first, place):
    rows = resid.shape[0]
    n, t, _, c, hid = pack.shape
    full = jax.ShapeDtypeStruct((rows, HW), f32)
    thin = jax.ShapeDtypeStruct((HW, TOKCH), f32)
    early = lambda s: jnp.minimum(s, t - 1)
    late = lambda s: jnp.maximum(s - t, 0)
    return pl.pallas_call(
        final_kernel,
        grid=(3 * t,),
        in_specs=[
            whole((rows, HW)),
            whole((rows, HW)),
            whole((rows, TOKCH)),
            whole((rows, 4)),
            whole((HW, TOKCH)),
            whole((HW, TOKCH)),
        ]
        + [pack_spec(pack, first + k, early) for k in range(2)]
        + [
            pl.BlockSpec(
                (n, 1, 1, c, hid), lambda s: (0, late(s) >> 1, first + (late(s) & 1), 0, 0)
            )
        ],
        out_specs=[
            out_whole((rows, HW)),
            out_whole((rows, HW)),
            pl.BlockSpec(
                (n, 1, 1, c, hid), lambda s: (0, late(s) >> 1, place + (late(s) & 1), 0, 0)
            ),
            out_whole((8, 128)),
            out_whole((HW, TOKCH)),
            out_whole((HW, TOKCH)),
        ],
        out_shape=[
            full,
            full,
            jax.ShapeDtypeStruct((n, t, place + 2, c, hid), bf16),
            jax.ShapeDtypeStruct((8, 128), f32),
            thin,
            thin,
        ],
        scratch_shapes=[pltpu.VMEM((rows, HW), f32)] * 4,
        compiler_params=params(),
        cost_estimate=cost(6 * rows * HW * 2 * HW, 8 * HW * HW + 20 * rows * HW),
    )(resid, cond, eps_true, coefs, w_mean, w_var, *[pack] * 3)


def condition_kernel(
    emb_ref, in_ref, wti_ref, wto_ref, wc_ref, tpre_ref, tact_ref, condition_ref, cond_ref
):
    time_pre = product(emb_ref[...], wti_ref[...])
    tpre_ref[...] = time_pre
    time_act = silu_pair(time_pre)[0].astype(bf16)
    tact_ref[...] = time_act
    time_emb = product(time_act, wto_ref[...])
    cond_pre = product(in_ref[...], wc_ref[...])
    masked = in_ref.shape[0]
    for c in range(COPIES):
        rows = slice(c * masked, (c + 1) * masked)
        condition_ref[rows, :] = time_emb[rows] + cond_pre
    cond_ref[...] = silu_pair(condition_ref[...])[0].astype(bf16)


def vmem_spec():
    return pl.BlockSpec(memory_space=pltpu.VMEM)


def condition_forward(embedded, cond_in, time_in_weight, time_out_weight, cond_weight):
    rows = embedded.shape[0]
    full = jax.ShapeDtypeStruct((rows, HW), f32)
    low = jax.ShapeDtypeStruct((rows, HW), bf16)
    return pl.pallas_call(
        condition_kernel,
        in_specs=[vmem_spec()] * 5,
        out_specs=[vmem_spec()] * 4,
        out_shape=[full, low, full, low],
        compiler_params=params(),
        cost_estimate=cost(2 * rows * HW * 2 * HW, 4 * HW * HW + 10 * rows * HW),
    )(embedded, cond_in, time_in_weight, time_out_weight, cond_weight)


def condition_back_kernel(
    gc_ref, condition_ref, tpre_ref, tact_ref, emb_ref, in_ref, wto_ref, wc_ref,
    gin_ref, dto_ref, dti_ref, dc_ref, gcond_s,
):
    gcond_s[...] = gc_ref[...] * silu_pair(condition_ref[...])[1]
    grad_temb = gcond_s[...].astype(bf16)
    masked = in_ref.shape[0]
    total = gcond_s[0:masked, :]
    for c in range(1, COPIES):
        total = total + gcond_s[c * masked : (c + 1) * masked, :]
    grad_cpre = total.astype(bf16)
    gin_ref[...] = product_nt(grad_cpre, wc_ref[...]).astype(bf16)
    dc_ref[...] = product_tn(in_ref[...], grad_cpre).astype(bf16)
    grad_tact = product_nt(grad_temb, wto_ref[...])
    dto_ref[...] = product_tn(tact_ref[...], grad_temb).astype(bf16)
    grad_tpre = (grad_tact * silu_pair(tpre_ref[...])[1]).astype(bf16)
    dti_ref[...] = product_tn(emb_ref[...], grad_tpre).astype(bf16)


def condition_backward(
    grad_cond, condition, time_pre, time_act, embedded, cond_in, time_out_weight, cond_weight
):
    rows = embedded.shape[0]
    return pl.pallas_call(
        condition_back_kernel,
        in_specs=[vmem_spec()] * 8,
        out_specs=[vmem_spec()] * 4,
        out_shape=[
            jax.ShapeDtypeStruct(cond_in.shape, bf16),
            jax.ShapeDtypeStruct((HW, HW), bf16),
            jax.ShapeDtypeStruct((embedded.shape[1], HW), bf16),
            jax.ShapeDtypeStruct((cond_in.shape[1], HW), bf16),
        ],
        scratch_shapes=[pltpu.VMEM((rows, HW), f32)],
        compiler_params=params(),
        cost_estimate=cost(rows, rows),
    )(
        grad_cond, condition, time_pre, time_act, embedded, cond_in, time_out_weight,
        cond_weight,
    )


def butterfly(values, axis):
    for bit in bit_list(lax.axis_size(axis)):
        values = values + flip(values, axis, bit)
    return values


def shards(
    tokens,
    segment_ids,
    visible,
    mask_index,
    targets,
    noise,
    timesteps,
    ln1_gain,
    ln1_bias,
    qkv_weight,
    proj_weight,
    ln2_gain,
    ln2_bias,
    fc_in_weight,
    fc_out_weight,
    cond_weight,
    time_in_weight,
    time_out_weight,
    input_weight,
    ada_weight,
    block_in_weight,
    block_out_weight,
    final_ada_weight,
    out_weight,
):
    t, z = lax.axis_size("tensor"), lax.axis_index("tensor")
    n, d = lax.axis_size("dp"), lax.axis_index("dp")
    token_count, model_width = tokens.shape
    local_width = qkv_weight.shape[2]
    head_count = local_width // HEAD
    hid = input_weight.shape[1]
    chunk_rows = HW // n
    score_scale = 1.0 / math.sqrt(HEAD)
    own_rows = token_count // t

    ada_chunk = lax.dynamic_slice_in_dim(ada_weight, d * chunk_rows, chunk_rows, 1)
    in_chunk = lax.dynamic_slice_in_dim(block_in_weight, d * chunk_rows, chunk_rows, 1)
    out_chunk = lax.dynamic_slice_in_dim(block_out_weight, d * chunk_rows, chunk_rows, 2)
    def layer_chunk(l):
        return [
            jnp.moveaxis(ada_chunk[l], 1, 0),
            in_chunk[l][None],
            out_chunk[l].T[None],
        ]

    final_chunk = lax.dynamic_slice_in_dim(final_ada_weight, d * chunk_rows, chunk_rows, 0)
    half_depth = DEPTH // 2
    first_pack = gather_pack(
        jnp.concatenate(sum([layer_chunk(l) for l in range(half_depth)], []), axis=0)
    )
    second_pack = gather_pack(
        jnp.concatenate(
            sum([layer_chunk(l) for l in range(half_depth, DEPTH)], [])
            + [jnp.moveaxis(final_chunk, 1, 0)],
            axis=0,
        )
    )

    def pack_of(l):
        return (first_pack, 5 * l) if l < half_depth else (second_pack, 5 * (l - half_depth))

    input_full = relabel(jnp.concatenate(gather_blocks(input_weight), axis=1), 1, t, z)
    out_full = relabel(jnp.concatenate(gather_blocks(out_weight), axis=0), 0, t, z)

    inputs = relabel(tokens, 0, t, z).astype(f32)
    segments = relabel(segment_ids[0], 0, t, z)
    shown_keys = relabel(visible[0], 0, t, z)
    normal_one, inverse_one = plain_norm(inputs)
    attn_in = (normal_one * ln1_gain + ln1_bias).astype(bf16)
    qkv_flat = qkv_weight.reshape(model_width, 3 * local_width)
    projected = product(attn_in, qkv_flat).astype(bf16)
    queries = projected[:, :local_width].reshape(token_count, head_count, HEAD)
    key_rows = projected[:, local_width : 2 * local_width].reshape(token_count, head_count, HEAD)
    value_rows = projected[:, 2 * local_width :].reshape(token_count, head_count, HEAD)
    positions = jnp.arange(token_count)
    allowed = (segments[:, None] == segments[None, :]) & (
        (shown_keys[None, :] == 1) | (positions[:, None] == positions[None, :])
    )
    scores = (
        jnp.einsum("qhd,khd->hqk", queries, key_rows, preferred_element_type=f32) * score_scale
    )
    scores = jnp.where(allowed[None], scores, -1e30)
    row_top = jnp.max(scores, axis=-1, keepdims=True)
    weights_exp = jnp.exp(scores - row_top)
    row_total = jnp.sum(weights_exp, axis=-1, keepdims=True)
    probability = weights_exp / row_total
    prob_low = probability.astype(bf16)
    attn_out = (
        jnp.einsum("hqk,khd->qhd", prob_low, value_rows, preferred_element_type=f32)
        .reshape(token_count, local_width)
        .astype(bf16)
    )

    def row_blocks(values):
        return [values[r * own_rows : (r + 1) * own_rows] for r in range(t)]

    middle = inputs[:own_rows] + scatter_sum(row_blocks(product(attn_out, proj_weight)))
    normal_two, inverse_two = plain_norm(middle)
    mlp_in = jnp.concatenate(
        gather_blocks((normal_two * ln2_gain + ln2_bias).astype(bf16)), axis=0
    )
    mlp_pre = product(mlp_in, fc_in_weight)
    activated = jax.nn.gelu(mlp_pre, approximate=False).astype(bf16)
    hidden = middle + scatter_sum(row_blocks(product(activated, fc_out_weight)))
    hidden_rel = jnp.concatenate(gather_blocks(hidden.astype(bf16)), axis=0)
    hidden_out = relabel(hidden_rel, 0, t, z)

    masked_count = mask_index.shape[1]
    own_masked = masked_count // t
    row_count = COPIES * own_masked
    index_all = mask_index[0]
    index_all = ((index_all // own_rows) ^ z) * own_rows + index_all % own_rows
    index_all = relabel(index_all, 0, t, z)
    cond_in = hidden_rel[index_all[:own_masked]]
    time_own = lax.dynamic_slice_in_dim(timesteps[:, 0], z * own_masked, own_masked, 1)
    time_flat = time_own.reshape(row_count)
    embedded = frequency(time_flat).astype(bf16)
    time_pre, time_act, condition, cond_act = condition_forward(
        embedded, cond_in, time_in_weight, time_out_weight, cond_weight
    )
    abar_now, alpha_step, beta_step, beta_tilde, one_minus_now = plan(time_flat[:, None])
    start_own = lax.dynamic_slice_in_dim(targets[0], z * own_masked, own_masked, 0)
    start_rows = jnp.broadcast_to(start_own[None], (COPIES, own_masked, TOKCH)).reshape(
        row_count, TOKCH
    )
    eps_true = lax.dynamic_slice_in_dim(noise[:, 0], z * own_masked, own_masked, 1).reshape(
        row_count, TOKCH
    )
    noisy_rows = (jnp.sqrt(abar_now) * start_rows + jnp.sqrt(one_minus_now) * eps_true).astype(bf16)
    residual = product(noisy_rows, input_full)

    stored = []
    for l in range(DEPTH):
        scale, gate, pre, mod, block_out, following = layer_forward(
            residual, cond_act, *pack_of(l)
        )
        stored.append((residual, scale, gate, pre, mod, block_out))
        residual = following
    coef_diff = beta_step / jnp.sqrt(one_minus_now * alpha_step)
    coefs = jnp.concatenate(
        [jnp.log(beta_step), jnp.log(beta_tilde), coef_diff, jnp.zeros_like(coef_diff)], axis=1
    )

    grad_resid, grad_cact, final_grads, loss_tile, mean_part, var_part = final_layer(
        residual,
        cond_act,
        eps_true,
        coefs,
        out_full[:, :TOKCH],
        out_full[:, TOKCH:],
        second_pack,
        5 * (DEPTH - half_depth),
        0,
    )
    loss_total = loss_tile[0, 0]
    out_weight_part = jnp.concatenate([mean_part, var_part], axis=1)

    cond_turned = cond_act.T
    buffers = []
    for group in GROUPS:
        grads = None
        for i, l in enumerate(group):
            grad_resid, grad_cact, grads = layer_backward(
                grad_resid, stored[l], cond_turned, grad_cact, *pack_of(l), grads, i, len(group)
            )
        buffers.append(grads)
    input_weight_part = product_tn(noisy_rows, grad_resid.astype(bf16))

    grad_cond_in, *thin = condition_backward(
        grad_cact, condition, time_pre, time_act, embedded, cond_in, time_out_weight, cond_weight
    )
    thin = jnp.concatenate([part.reshape(n, part.shape[0] // n, HW) for part in thin], axis=1)
    thin = relabel(thin, 0, n, d)
    thin_red = reduce_dp(thin[::2], thin[1::2])
    for bit in bit_list(t):
        thin_low = thin_red.astype(bf16)
        thin_red = thin_low.astype(f32) + flip(thin_low, "tensor", bit).astype(f32)
    marks = [HW // n, HW // n + FREQ // n]
    time_out_grad, time_in_grad, cond_grad = jnp.split(thin_red, marks, axis=0)

    grad_in_all = jnp.concatenate(gather_blocks(grad_cond_in), axis=0)
    grad_mlp = jnp.zeros((token_count, model_width), bf16).at[index_all].add(grad_in_all)
    grad_act_mlp = product_nt(grad_mlp, fc_out_weight)
    grad_mlp_pre = jax.vjp(partial(jax.nn.gelu, approximate=False), mlp_pre)[1](grad_act_mlp)[
        0
    ].astype(bf16)
    grad_normed_two = scatter_sum(row_blocks(product_nt(grad_mlp_pre, fc_in_weight)))
    ln2_gain_part = jnp.sum(grad_normed_two * normal_two, axis=0)
    ln2_bias_part = jnp.sum(grad_normed_two, axis=0)
    grad_middle = grad_mlp[:own_rows].astype(f32) + norm_back(
        grad_normed_two * ln2_gain, normal_two, inverse_two
    )
    grad_attn = jnp.concatenate(gather_blocks(grad_middle.astype(bf16)), axis=0)
    grad_attn_out = (
        product_nt(grad_attn, proj_weight).astype(bf16).reshape(token_count, head_count, HEAD)
    )
    value_grad = jnp.einsum("hqk,qhd->khd", prob_low, grad_attn_out, preferred_element_type=f32)
    grad_prob = jnp.einsum("qhd,khd->hqk", grad_attn_out, value_rows, preferred_element_type=f32)
    row_delta = jnp.sum(probability * grad_prob, axis=-1, keepdims=True)
    grad_scores = (probability * (grad_prob - row_delta)).astype(bf16)
    query_grad = (
        jnp.einsum("hqk,khd->qhd", grad_scores, key_rows, preferred_element_type=f32) * score_scale
    )
    key_grad = (
        jnp.einsum("hqk,qhd->khd", grad_scores, queries, preferred_element_type=f32) * score_scale
    )
    grad_qkv = jnp.concatenate(
        [
            query_grad.reshape(token_count, local_width),
            key_grad.reshape(token_count, local_width),
            value_grad.reshape(token_count, local_width),
        ],
        axis=1,
    ).astype(bf16)
    grad_normed_one = scatter_sum(row_blocks(product_nt(grad_qkv, qkv_flat)))
    own_normal = normal_one[:own_rows]
    ln1_gain_part = jnp.sum(grad_normed_one * own_normal, axis=0)
    ln1_bias_part = jnp.sum(grad_normed_one, axis=0)
    input_own = grad_middle + norm_back(
        grad_normed_one * ln1_gain, own_normal, inverse_one[:own_rows]
    )
    input_grad = relabel(
        jnp.concatenate(gather_blocks(input_own.astype(bf16)), axis=0), 0, t, z
    ).astype(f32)

    final_part = reduce_over_dp(final_grads)
    final_grad = jnp.moveaxis(reduce_tensor(final_part, z), 0, 1)
    parts = [reduce_over_dp(buffers[0])]
    parts += [reduce_over_dp(after(buffer, parts[0], query_grad)) for buffer in buffers[1:]]
    reds = [None] * DEPTH
    for group, part in zip(GROUPS, parts):
        group_sum = reduce_tensor(part, z)
        for i, l in enumerate(group):
            reds[l] = group_sum[5 * i : 5 * i + 5]
    ada_grad = jnp.stack([jnp.moveaxis(red[:3], 0, 1) for red in reds])
    in_grad = jnp.stack([red[3] for red in reds])
    out_grad = jnp.stack([red[4].T for red in reds])

    whole_grads = jnp.concatenate(
        [
            product_tn(attn_in, grad_qkv),
            product_tn(grad_attn, attn_out),
            product_tn(mlp_in, grad_mlp_pre),
            product_tn(grad_mlp, activated),
        ],
        axis=1,
    )
    whole_grads = relabel(
        whole_grads.astype(bf16).reshape(n, model_width // n, whole_grads.shape[1]), 0, n, d
    )
    block_red = reduce_dp(whole_grads[::2], whole_grads[1::2])
    marks = [3 * local_width, 4 * local_width, 4 * local_width + fc_in_weight.shape[1]]
    qkv_red, proj_red, fc_in_red, fc_out_red = jnp.split(block_red, marks, axis=1)

    lane_parts = jnp.concatenate(
        [
            ln1_gain_part,
            ln1_bias_part,
            ln2_gain_part,
            ln2_bias_part,
            jnp.full((128,), loss_total, f32),
        ]
    )
    input_weight_part = relabel(input_weight_part, 1, t, z)
    out_weight_part = relabel(out_weight_part, 0, t, z)
    shard_parts = [
        jnp.concatenate(
            [
                input_weight_part[:, r * hid : (r + 1) * hid].reshape(-1),
                out_weight_part[r * hid : (r + 1) * hid].reshape(-1),
            ]
        )
        for r in range(t)
    ]
    shard_own = shard_parts[0]
    for r in range(1, t):
        shard_own = shard_own + flip(shard_parts[r], "tensor", r)
    small = butterfly(jnp.concatenate([butterfly(lane_parts, "tensor"), shard_own]), "dp")
    lanes = 4 * model_width + 128
    edge = lanes + TOKCH * hid
    loss_mean = small[4 * model_width] / (n * t * row_count)
    return (
        loss_mean,
        hidden_out,
        input_grad,
        small[:model_width],
        small[model_width : 2 * model_width],
        qkv_red.reshape(model_width // n, 3, local_width),
        proj_red.T,
        small[2 * model_width : 3 * model_width],
        small[3 * model_width : 4 * model_width],
        fc_in_red,
        fc_out_red.T,
        cond_grad,
        time_in_grad,
        time_out_grad,
        small[lanes:edge].reshape(TOKCH, hid),
        ada_grad,
        in_grad,
        out_grad,
        final_grad,
        small[edge:].reshape(out_weight.shape),
    )


def solution(mesh):
    placed = (
        P("dp", None),
        P("dp", None),
        P("dp", None),
        P("dp", None),
        P("dp", None, None),
        P(None, "dp", None, None),
        P(None, "dp", None),
        P(),
        P(),
        P(None, None, "tensor"),
        P("tensor", None),
        P(),
        P(),
        P(None, "tensor"),
        P("tensor", None),
        P(),
        P(),
        P(),
        P(None, "tensor"),
        P(None, None, None, "tensor"),
        P(None, None, "tensor"),
        P(None, "tensor", None),
        P(None, None, "tensor"),
        P("tensor", None),
    )
    return jax.shard_map(
        shards,
        mesh=mesh,
        in_specs=placed,
        out_specs=(
            P(),
            P("dp", None),
            P("dp", None),
            P(),
            P(),
            P("dp", None, "tensor"),
            P("tensor", "dp"),
            P(),
            P(),
            P("dp", "tensor"),
            P("tensor", "dp"),
            P("dp", None),
            P("dp", None),
            P("dp", None),
            P(None, "tensor"),
            P(None, "dp", None, "tensor"),
            P(None, "dp", "tensor"),
            P(None, "tensor", "dp"),
            P("dp", None, "tensor"),
            P("tensor", None),
        ),
        check_vma=False,
    )
```
